256 devices in a mesh: grp: 64 (over y, z, core), dir: 4 (over x).
Axes of the slice: x: 4, y: 4, z: 8, core: 2. Of those that a mesh axis runs over, the one named last changes fastest.
Arguments:
- currents: bfloat16 [16384, 128], P('grp'), may hold values from -6 to 6
- basis_group: int32 [16384], P('grp'), may hold values from 0 to 1
- projection: bfloat16 [16384, 1024], P('grp', 'dir'), may hold values from -0.5 to 0.5
- filters: bfloat16 [4, 64, 1024], P(None, None, 'dir'), may hold values from -0.09375 to 0.09375
- pair_src: int32 [8192], P('grp'), may hold values from 0 to 63, as said below
- pair_dst: int32 [8192], P('grp'), may hold values from 0 to 63, as said below
- pair_type: int32 [8192], P('grp'), may hold values from 0 to 3
- live_count: int32 [64], P('grp'), may hold values from 64 to 128, as said below
- send_group: int32 [64, 64], replicated, may hold values from 0 to 1, as said below
- recv_group: int32 [64, 64], replicated, may hold values from 0 to 1, as said below
Outputs:
- field: bfloat16 [16384, 128], P('grp')
The draws below stay inside these ranges and needn't reach their ends.
Inputs may be any that keep to these rules, and one draw needn't show every extreme that they name: `pair_src`: for each reader, its first 64 slots name every owner once. `pair_dst`: for each reader, its first 64 slots name every owner once. `live_count`: some reader has all 128 slots live. `send_group`: each row names every one of the owner's groups at least once. `recv_group`: each row names every one of the owner's groups at least once.
All inputs are finite; a program needn't handle non-finite values.
Results may differ from the reference program's by a relative error of at most 0.0058.
Values may be sent and summed in bfloat16 or wider, within the bound.
A program may use at most 192 MiB of HBM per device.

```python
import jax
import jax.numpy as jnp
from jax import lax

K = 1024
TAPS = 64
BPG = 128
G_DEV = 2
TYPES = 4
READERS = 64
FAR_DEV = 128
NT = 128
GROUPS = 128
BASIS = 16384


def pair_rows(key, salt):
    keys = jax.random.split(jax.random.fold_in(key, salt), READERS)

    def single_row(row_key):
        first_key, second_key = jax.random.split(row_key)
        head = jax.random.permutation(first_key, READERS).astype(jnp.int32)
        tail = jax.random.randint(second_key, (FAR_DEV - READERS,), 0, READERS).astype(jnp.int32)
        return jnp.concatenate([head, tail])
    return jax.vmap(single_row)(keys).reshape(-1)


def owner_table(key, salt):
    keys = jax.random.split(jax.random.fold_in(key, salt), READERS)

    def single_owner(owner_key):
        first_key, second_key = jax.random.split(owner_key)
        base = jax.random.randint(first_key, (READERS,), 0, G_DEV).astype(jnp.int32)
        places = jax.random.permutation(second_key, READERS)[:G_DEV]
        return base.at[places].set(jnp.arange(G_DEV, dtype=jnp.int32))
    return jax.vmap(single_owner)(keys)


def draw_pair_src(key, part):
    return pair_rows(key, 11)


def draw_pair_dst(key, part):
    return pair_rows(key, 23)


def draw_live_count(key, part):
    first_key, second_key, third_key, fourth_key = jax.random.split(jax.random.fold_in(key, 31), 4)
    span = FAR_DEV - READERS + 1
    extra = jax.random.randint(first_key, (READERS,), 0, span)
    extra = jnp.minimum(extra, jax.random.randint(second_key, (READERS,), 0, span))
    extra = jnp.minimum(extra, jax.random.randint(third_key, (READERS,), 0, span))
    counts = (READERS + extra).astype(jnp.int32)
    heaviest_group = jax.random.randint(fourth_key, (), 0, READERS)
    return counts.at[heaviest_group].set(FAR_DEV)


def draw_send_group(key, part):
    return owner_table(key, 37)


def draw_recv_group(key, part):
    return owner_table(key, 41)


def plant(values, stream_key, least, largest):
    spot = [jax.random.randint(jax.random.fold_in(stream_key, axis), (), 0, length) for axis, length in enumerate(values.shape)]
    widest = values.shape.index(max(values.shape))
    next_to = spot[:widest] + [(spot[widest] + 1) % values.shape[widest]] + spot[widest + 1:]
    return values.at[tuple(spot)].set(least).at[tuple(next_to)].set(largest)


def steps_of(own_key, dims, cuts, least, high):
    factor_of = 1.0
    for position, parts in cuts:
        steps = jax.random.uniform(jax.random.fold_in(jax.random.fold_in(own_key, 6), position), (parts,), jnp.float32, least / len(cuts), high / len(cuts))
        factor_of = factor_of * jnp.repeat(jnp.exp(steps), dims[position] // parts).reshape((-1,) + (1,) * (len(dims) - 1 - position))
    return factor_of


def bell_draw(key, shape, deviation, reach, shards=(), kind=jnp.bfloat16):
    drawn = deviation * jax.random.normal(key, shape, jnp.float32)
    if shards:
        drawn = drawn * steps_of(key, shape, shards, -0.22, 0.18)
    return jnp.clip(drawn, -reach, reach).astype(kind)


def setup_inputs(seed: int = 0) -> dict:
    key_of = jax.random.split(jax.random.key(seed), 11)
    return {
        "currents": bell_draw(key_of[0], (BASIS, NT), 1.0, 6.0, ((0, 64),)),
        "basis_group": plant(jax.random.randint(key_of[1], (BASIS,), 0, G_DEV), jax.random.fold_in(key_of[1], 1), 0, G_DEV - 1).astype(jnp.int32),
        "projection": bell_draw(key_of[2], (BASIS, K), BPG ** -0.5, 0.5, ((0, 64), (1, 4))),
        "filters": bell_draw(key_of[3], (TYPES, TAPS, K), (TAPS * FAR_DEV // G_DEV) ** -0.5, 0.09375, ((2, 4),)),
        "pair_src": draw_pair_src(jax.random.fold_in(key_of[10], 71), 0),
        "pair_dst": draw_pair_dst(jax.random.fold_in(key_of[10], 71), 0),
        "pair_type": plant(jax.random.randint(key_of[6], (READERS * FAR_DEV,), 0, TYPES), jax.random.fold_in(key_of[6], 1), 0, TYPES - 1).astype(jnp.int32),
        "live_count": draw_live_count(jax.random.fold_in(key_of[10], 71), 0),
        "send_group": draw_send_group(jax.random.fold_in(key_of[10], 71), 0),
        "recv_group": draw_recv_group(jax.random.fold_in(key_of[10], 71), 0),
    }


def reference(currents, basis_group, projection, filters, pair_src, pair_dst, pair_type, live_count, send_group, recv_group):
    device_rows = BPG * G_DEV
    labels = jnp.arange(G_DEV, dtype=jnp.int32)
    currents_dev = currents.reshape(READERS, device_rows, NT)
    pattern_dev = projection.reshape(READERS, device_rows, K)
    member_device = basis_group.reshape(READERS, device_rows)

    def project(inputs):
        series, pattern, member = inputs
        onehot = (member[:, None] == labels[None, :]).astype(jnp.float32)
        spread = series.astype(jnp.float32)[:, None, :] * onehot[:, :, None]
        return jnp.einsum("bk,bgt->gkt", pattern.astype(jnp.float32), spread, precision=lax.Precision.HIGHEST)

    signature = lax.map(project, (currents_dev, pattern_dev, member_device))
    signature = signature.reshape(GROUPS, K, NT).astype(jnp.bfloat16)

    rows = jnp.arange(READERS * FAR_DEV, dtype=jnp.int32)
    reader = rows // FAR_DEV
    slot = rows % FAR_DEV
    live = slot < live_count[reader]
    source = pair_src * G_DEV + send_group[pair_src, reader]
    target = pair_dst * G_DEV + recv_group[pair_dst, reader]
    delay_bucket = target * TYPES + pair_type

    def add_reader(store, inputs):
        source_row, bucket_row, live_row = inputs
        values = jnp.take(signature, source_row, axis=0).astype(jnp.float32)
        values = values * live_row.astype(jnp.float32)[:, None, None]
        return store.at[bucket_row].add(values), None

    store = jnp.zeros((GROUPS * TYPES, K, NT), dtype=jnp.float32)
    store, _ = lax.scan(add_reader, store, (source.reshape(READERS, FAR_DEV), delay_bucket.reshape(READERS, FAR_DEV), live.reshape(READERS, FAR_DEV)))
    store = store.reshape(GROUPS, TYPES, K, NT)

    times = jnp.arange(NT, dtype=jnp.int32)
    delay = times[None, :] - times[:, None]
    valid = (delay >= 0) & (delay < TAPS)
    lag_index = jnp.clip(delay, 0, TAPS - 1)
    toeplitz = jnp.take(filters.astype(jnp.float32), lag_index, axis=1)
    toeplitz = jnp.where(valid[None, :, :, None], toeplitz, jnp.zeros_like(toeplitz))
    incoming = jnp.einsum("gcks,cstk->gkt", store, toeplitz, precision=lax.Precision.HIGHEST)
    incoming = incoming.astype(jnp.bfloat16).reshape(READERS, G_DEV, K, NT)

    def disaggregate(inputs):
        pattern, member, arriving = inputs
        onehot = (member[:, None] == labels[None, :]).astype(jnp.float32)
        spread = jnp.einsum("bk,gkt->bgt", pattern.astype(jnp.float32), arriving.astype(jnp.float32), precision=lax.Precision.HIGHEST)
        return jnp.sum(spread * onehot[:, :, None], axis=1)

    field = lax.map(disaggregate, (pattern_dev, member_device, incoming))
    return field.reshape(BASIS, NT).astype(jnp.bfloat16)
```

```python
import functools

import jax
import jax.numpy as jnp
from jax import lax
from jax.experimental import pallas as pl
from jax.experimental.pallas import tpu as pltpu
from jax.sharding import PartitionSpec as P

MESH = pl.DeviceIdType.MESH
F32 = jnp.float32
BF16 = jnp.bfloat16
TYPES = 4
GROUPS_OWN = 2
KD = 4
NTAB = 8
READER_CHUNK = 8


def dot_nt(a, b):
    return lax.dot_general(a, b, (((1,), (1,)), ((), ())), preferred_element_type=F32)


def dot(a, b):
    return jnp.dot(a, b, preferred_element_type=F32)


def iota(shape, axis):
    return lax.broadcasted_iota(jnp.int32, shape, axis)


def kernel(
    n,
    nd,
    taps,
    cur_h,
    bg_h,
    proj_h,
    filt_h,
    src_h,
    dst_h,
    typ_h,
    live_h,
    sg_h,
    rg_h,
    out_h,
    cur,
    bg,
    proj,
    filt,
    src,
    dst,
    typ,
    live,
    sg,
    rg,
    local_sems,
    tab_send,
    tab_recv,
    sig_send,
    sig_recv,
    in_send,
    in_recv,
    term_send,
    term_recv,
    fin_send,
    send_sems,
    recv_sems,
    out_sem,
    pattern,
    back,
    toep,
    index_b,
    index_s,
    rows_f,
):
    p = lax.axis_index("grp")
    d = lax.axis_index("dir")
    rows, steps = cur.shape
    slots = src.shape[1]
    groups = GROUPS_OWN * n
    share = rows // nd

    locals_ = []
    for i, (a, b) in enumerate(
        [
            (src_h, src),
            (dst_h, dst),
            (typ_h, typ),
            (live_h, live),
            (sg_h, sg),
            (rg_h, rg),
            (proj_h, proj),
            (cur_h, cur),
            (bg_h, bg),
            (filt_h, filt),
        ]
    ):
        copy = pltpu.make_async_copy(a, b, local_sems.at[i])
        copy.start()
        locals_.append(copy)

    barrier = pltpu.get_barrier_semaphore()

    def greet(i, carry):
        pl.semaphore_signal(barrier, 1, device_id=(lax.rem(p + i, n), d), device_id_type=MESH)
        return carry

    lax.fori_loop(1, n, greet, 0)
    for i in range(1, nd):
        pl.semaphore_signal(barrier, 1, device_id=(p, lax.rem(d + i, nd)), device_id_type=MESH)

    for copy in locals_[:6]:
        copy.wait()
    owners = iota((n, slots), 0)
    here = iota((n, n), 1) == p
    send_col = jnp.sum(jnp.where(here, sg[...].astype(F32), 0.0), axis=1, keepdims=True)
    recv_col = jnp.sum(jnp.where(here, rg[...].astype(F32), 0.0), axis=1, keepdims=True)
    send_of = jnp.sum(jnp.where(owners == src[...], send_col, 0.0), axis=0, keepdims=True)
    recv_of = jnp.sum(jnp.where(owners == dst[...], recv_col, 0.0), axis=0, keepdims=True)
    source = send_of * n + src[...].astype(F32)
    target = recv_of * n + dst[...].astype(F32)
    is_live = jnp.where(iota((1, slots), 1) < live[...], 1.0, 0.0)
    row = iota((NTAB, slots), 0)
    table = jnp.where(
        row == 0,
        source,
        jnp.where(
            row == 1, target, jnp.where(row == 2, typ[...].astype(F32), jnp.where(row == 3, is_live, 0.0))
        ),
    )
    tab_send[...] = table.astype(BF16)
    tab_recv[pl.ds(p, 1)] = table.astype(BF16)[None]

    for copy in locals_[6:9]:
        copy.wait()
    width = proj.shape[1]
    pick = (iota((GROUPS_OWN * width, width), 0) // GROUPS_OWN == iota((GROUPS_OWN * width, width), 1))
    spread = dot_nt(pick.astype(F32).astype(BF16), proj[...])
    owned = lax.rem(iota((GROUPS_OWN * width, rows), 0), GROUPS_OWN) == bg[...]
    pattern[...] = jnp.where(owned, spread, 0.0).astype(BF16)
    signature = dot(pattern[...], cur[...])
    sig_send[...] = signature.reshape(n, GROUPS_OWN * KD, steps).astype(BF16)
    sig_recv[pl.ds(p, 1)] = sig_send[pl.ds(p, 1)]

    pl.semaphore_wait(barrier, n - 1 + nd - 1)

    def send_table(i, carry):
        peer = lax.rem(p + i, n)
        pltpu.make_async_remote_copy(
            src_ref=tab_send,
            dst_ref=tab_recv.at[p],
            send_sem=send_sems.at[0],
            recv_sem=recv_sems.at[0],
            device_id=(peer, d),
            device_id_type=MESH,
        ).start()
        return carry

    def send_signature(i, carry):
        peer = lax.rem(p + i, n)
        pltpu.make_async_remote_copy(
            src_ref=sig_send.at[peer],
            dst_ref=sig_recv.at[p],
            send_sem=send_sems.at[1],
            recv_sem=recv_sems.at[1],
            device_id=(peer, d),
            device_id_type=MESH,
        ).start()
        return carry

    lax.fori_loop(1, n, send_table, 0)
    lax.fori_loop(1, n, send_signature, 0)

    def await_bytes(ref, sem):
        pltpu.make_async_copy(ref, ref, sem).wait()

    eye = (iota((rows, rows), 0) == iota((rows, rows), 1)).astype(F32).astype(BF16)
    back[...] = dot_nt(eye, pattern[...]).astype(BF16)
    locals_[9].wait()
    mine = (iota((8, width), 1) == iota((8, width), 0) + KD * p) & (iota((8, width), 0) < KD)
    tap_rows = dot_nt(mine.astype(F32).astype(BF16), filt[...])
    lag = iota((steps, steps), 1) - iota((steps, steps), 0)
    causal = (lag >= 0) & (lag < taps)
    for k in range(KD):
        for c in range(TYPES):
            first = c * taps
            base = first // steps * steps
            line = jnp.broadcast_to(tap_rows[k : k + 1, base : base + steps], (steps, steps))
            turned = pltpu.roll(line, (steps - (first - base)) % steps, 1, stride=1, stride_axis=0)
            toep[k, c * steps : (c + 1) * steps, :] = jnp.where(causal, turned, 0.0).astype(BF16)

    await_bytes(tab_recv.at[pl.ds(0, n - 1)], recv_sems.at[0])
    tables = tab_recv[...].astype(F32)
    kind = tables[:, 2, :]
    high = jnp.where(kind >= 2.0, 1.0, 0.0)
    index_b[...] = jnp.where(tables[:, 3, :] > 0.0, high * groups + tables[:, 1, :], -1.0)
    index_s[...] = (kind - 2.0 * high) * groups + tables[:, 0, :]
    wide = iota((2 * groups, slots), 0).astype(F32)

    def count_readers(step, total):
        hot_b, hot_s = [], []
        for j in range(READER_CHUNK):
            r = step * READER_CHUNK + j
            hot_b.append(jnp.where(wide == index_b[pl.ds(r, 1), :], 1.0, 0.0).astype(BF16))
            hot_s.append(jnp.where(wide == index_s[pl.ds(r, 1), :], 1.0, 0.0).astype(BF16))
        return total + dot_nt(jnp.concatenate(hot_b, axis=1), jnp.concatenate(hot_s, axis=1))

    count = lax.fori_loop(
        0, n // READER_CHUNK, count_readers, jnp.zeros((2 * groups, 2 * groups), F32)
    )
    hundreds = jnp.floor(count * (1.0 / 256.0))
    units = count - 256.0 * hundreds
    parts = []
    for c in range(TYPES):
        r0, c0 = c // 2 * groups, c % 2 * groups
        parts.append(
            jnp.concatenate(
                [
                    units[r0 : r0 + groups, c0 : c0 + groups],
                    hundreds[r0 : r0 + groups, c0 : c0 + groups],
                ],
                axis=1,
            )
        )
    counts = jnp.concatenate(parts, axis=0).astype(BF16)

    await_bytes(sig_recv.at[pl.ds(0, n - 1)], recv_sems.at[1])
    rows_f[...] = sig_recv[...].astype(F32)
    by_k = []
    for k in range(KD):
        by_k.append(
            jnp.concatenate([rows_f[:, GROUPS_OWN * k + g, :] for g in range(GROUPS_OWN)], axis=0)
        )
    signal = jnp.concatenate(by_k, axis=1)
    signal = jnp.concatenate([signal, 256.0 * signal], axis=0).astype(BF16)
    summed = dot(counts, signal)
    for k in range(KD):
        part = summed[:, k * steps : (k + 1) * steps]
        part = jnp.concatenate([part[c * groups : (c + 1) * groups] for c in range(TYPES)], axis=1)
        upper = part.astype(BF16)
        lower = (part - upper.astype(F32)).astype(BF16)
        both = dot(jnp.concatenate([upper, lower], axis=0), toep[k])
        arriving = both[:groups] + both[groups:]
        for g in range(GROUPS_OWN):
            rows_f[:, GROUPS_OWN * k + g, :] = arriving[g * n : (g + 1) * n]
    in_send[...] = rows_f[...].astype(BF16)
    in_recv[pl.ds(p, 1)] = in_send[pl.ds(p, 1)]

    def send_incoming(i, carry):
        peer = lax.rem(p + i, n)
        pltpu.make_async_remote_copy(
            src_ref=in_send.at[peer],
            dst_ref=in_recv.at[p],
            send_sem=send_sems.at[2],
            recv_sem=recv_sems.at[2],
            device_id=(peer, d),
            device_id_type=MESH,
        ).start()
        return carry

    lax.fori_loop(1, n, send_incoming, 0)
    await_bytes(in_recv.at[pl.ds(0, n - 1)], recv_sems.at[2])

    incoming = in_recv[...].astype(F32).reshape(n * GROUPS_OWN * KD, steps).astype(BF16)
    term_send[...] = dot(back[...], incoming).reshape(nd, share, steps)
    term_recv[pl.ds(d, 1)] = term_send[pl.ds(d, 1)]
    for i in range(1, nd):
        peer = lax.rem(d + i, nd)
        pltpu.make_async_remote_copy(
            src_ref=term_send.at[peer],
            dst_ref=term_recv.at[d],
            send_sem=send_sems.at[3],
            recv_sem=recv_sems.at[3],
            device_id=(p, peer),
            device_id_type=MESH,
        ).start()
    await_bytes(term_recv.at[pl.ds(0, nd - 1)], recv_sems.at[3])
    total = term_recv[0]
    for i in range(1, nd):
        total = total + term_recv[i]
    fin_send[...] = total.astype(BF16)
    own = pltpu.make_async_copy(fin_send, out_h.at[d], out_sem)
    own.start()
    for i in range(1, nd):
        peer = lax.rem(d + i, nd)
        pltpu.make_async_remote_copy(
            src_ref=fin_send,
            dst_ref=out_h.at[d],
            send_sem=send_sems.at[4],
            recv_sem=recv_sems.at[4],
            device_id=(p, peer),
            device_id_type=MESH,
        ).start()
    await_bytes(tab_recv.at[pl.ds(0, n - 1)], send_sems.at[0])
    await_bytes(sig_send.at[pl.ds(0, n - 1)], send_sems.at[1])
    await_bytes(in_send.at[pl.ds(0, n - 1)], send_sems.at[2])
    await_bytes(term_send.at[pl.ds(0, nd - 1)], send_sems.at[3])
    own.wait()
    await_bytes(out_h.at[pl.ds(0, nd - 1)], send_sems.at[4])
    await_bytes(out_h.at[pl.ds(0, nd - 1)], recv_sems.at[4])


def local(
    currents,
    basis_group,
    projection,
    filters,
    pair_src,
    pair_dst,
    pair_type,
    live_count,
    send_group,
    recv_group,
):
    n = lax.axis_size("grp")
    nd = lax.axis_size("dir")
    rows, steps = currents.shape
    width = projection.shape[1]
    taps = filters.shape[1]
    slots = pair_src.shape[0]
    groups = GROUPS_OWN * n
    msg = GROUPS_OWN * KD
    any_space = pl.BlockSpec(memory_space=pltpu.HBM)
    out = pl.pallas_call(
        functools.partial(kernel, n, nd, taps),
        out_shape=jax.ShapeDtypeStruct((nd, rows // nd, steps), BF16),
        in_specs=[any_space] * 10,
        out_specs=any_space,
        scratch_shapes=[
            pltpu.VMEM((rows, steps), BF16),
            pltpu.VMEM((1, rows), jnp.int32),
            pltpu.VMEM((rows, width), BF16),
            pltpu.VMEM((TYPES * taps, width), BF16),
            pltpu.VMEM((1, slots), jnp.int32),
            pltpu.VMEM((1, slots), jnp.int32),
            pltpu.VMEM((1, slots), jnp.int32),
            pltpu.VMEM((1, 1), jnp.int32),
            pltpu.VMEM((n, n), jnp.int32),
            pltpu.VMEM((n, n), jnp.int32),
            pltpu.SemaphoreType.DMA((10,)),
            pltpu.VMEM((NTAB, slots), BF16),
            pltpu.VMEM((n, NTAB, slots), BF16),
            pltpu.VMEM((n, msg, steps), BF16),
            pltpu.VMEM((n, msg, steps), BF16),
            pltpu.VMEM((n, msg, steps), BF16),
            pltpu.VMEM((n, msg, steps), BF16),
            pltpu.VMEM((nd, rows // nd, steps), F32),
            pltpu.VMEM((nd, rows // nd, steps), F32),
            pltpu.VMEM((rows // nd, steps), BF16),
            pltpu.SemaphoreType.DMA((5,)),
            pltpu.SemaphoreType.DMA((5,)),
            pltpu.SemaphoreType.DMA,
            pltpu.VMEM((GROUPS_OWN * width, rows), BF16),
            pltpu.VMEM((rows, GROUPS_OWN * width), BF16),
            pltpu.VMEM((KD, TYPES * steps, steps), BF16),
            pltpu.VMEM((n, slots), F32),
            pltpu.VMEM((n, slots), F32),
            pltpu.VMEM((n, msg, steps), F32),
        ],
        compiler_params=pltpu.CompilerParams(
            collective_id=0, has_side_effects=True, vmem_limit_bytes=32 * 1024 * 1024
        ),
        name="far_field",
    )(
        currents,
        basis_group.reshape(1, rows),
        projection,
        filters.reshape(TYPES * taps, width),
        pair_src.reshape(1, slots),
        pair_dst.reshape(1, slots),
        pair_type.reshape(1, slots),
        live_count.reshape(1, 1),
        send_group,
        recv_group,
    )
    return out.reshape(rows, steps)


def solution(mesh):
    return jax.shard_map(
        local,
        mesh=mesh,
        in_specs=(
            P("grp", None),
            P("grp"),
            P("grp", "dir"),
            P(None, None, "dir"),
            P("grp"),
            P("grp"),
            P("grp"),
            P("grp"),
            P(),
            P(),
        ),
        out_specs=P("grp", None),
        check_vma=False,
    )
```

```python
import functools

import jax
import jax.numpy as jnp
from jax import lax
from jax.experimental import pallas as pl
from jax.experimental.pallas import tpu as pltpu
from jax.sharding import PartitionSpec as P

MESH = pl.DeviceIdType.MESH
F32 = jnp.float32
BF16 = jnp.bfloat16
TYPES = 4
GROUPS_OWN = 2
HALVES = 1
KH = 4
ROWS = GROUPS_OWN * KH
NTAB = 4
READER_CHUNK = 8


def dot_nt(a, b):
    return lax.dot_general(a, b, (((1,), (1,)), ((), ())), preferred_element_type=F32)


def dot(a, b):
    return jnp.dot(a, b, preferred_element_type=F32)


def iota(shape, axis):
    return lax.broadcasted_iota(jnp.int32, shape, axis)


def kernel(
    n,
    nd,
    taps,
    cur_h,
    bg_h,
    proj_h,
    filt_h,
    src_h,
    dst_h,
    typ_h,
    live_h,
    sg_h,
    rg_h,
    out,
    cur,
    bg,
    proj,
    filt,
    src,
    dst,
    typ,
    live,
    sg,
    rg,
    local_sems,
    tab_send,
    tab_recv,
    sig_send,
    sig_recv,
    in_send,
    in_recv,
    term_send,
    term_recv,
    send_sems,
    recv_sems,
    pattern,
    back,
    toep,
    index_b,
    index_s,
    rows_f,
):
    p = lax.axis_index("grp")
    d = lax.axis_index("dir")
    rows, steps = cur.shape
    slots = src.shape[1]
    groups = GROUPS_OWN * n

    locals_ = []
    for i, (a, b) in enumerate(
        [
            (src_h, src),
            (dst_h, dst),
            (typ_h, typ),
            (live_h, live),
            (sg_h, sg),
            (rg_h, rg),
            (proj_h, proj),
            (cur_h, cur),
            (bg_h, bg),
            (filt_h, filt),
        ]
    ):
        copy = pltpu.make_async_copy(a, b, local_sems.at[i])
        copy.start()
        locals_.append(copy)

    barrier = pltpu.get_barrier_semaphore()

    def greet(i, carry):
        pl.semaphore_signal(barrier, 1, device_id=(lax.rem(p + i, n), d), device_id_type=MESH)
        return carry

    lax.fori_loop(1, n, greet, 0)
    for i in range(1, nd):
        pl.semaphore_signal(barrier, 1, device_id=(p, lax.rem(d + i, nd)), device_id_type=MESH)

    for copy in locals_[:6]:
        copy.wait()
    owners = iota((n, slots), 0)
    here = iota((n, n), 1) == p
    send_col = jnp.sum(jnp.where(here, sg[...].astype(F32), 0.0), axis=1, keepdims=True)
    recv_col = jnp.sum(jnp.where(here, rg[...].astype(F32), 0.0), axis=1, keepdims=True)
    send_of = jnp.sum(jnp.where(owners == src[...], send_col, 0.0), axis=0, keepdims=True)
    recv_of = jnp.sum(jnp.where(owners == dst[...], recv_col, 0.0), axis=0, keepdims=True)
    source = send_of * n + src[...].astype(F32)
    target = recv_of * n + dst[...].astype(F32)
    is_live = jnp.where(iota((1, slots), 1) < live[...], 1.0, 0.0)
    row = iota((NTAB, slots), 0)
    table = jnp.where(
        row == 0,
        source,
        jnp.where(row == 1, target, jnp.where(row == 2, typ[...].astype(F32), is_live)),
    )
    tab_send[...] = table.astype(BF16)
    tab_recv[pl.ds(p, 1)] = table.astype(BF16)[None]

    for copy in locals_[6:9]:
        copy.wait()
    width = proj.shape[1]
    pick = (iota((GROUPS_OWN * width, width), 0) // GROUPS_OWN == iota((GROUPS_OWN * width, width), 1))
    spread = dot_nt(pick.astype(F32).astype(BF16), proj[...])
    owned = lax.rem(iota((GROUPS_OWN * width, rows), 0), GROUPS_OWN) == bg[...]
    pattern[...] = jnp.where(owned, spread, 0.0).astype(BF16)
    signature = dot(pattern[...], cur[...])
    sig_send[...] = signature.reshape(HALVES, n, ROWS, steps).astype(BF16)
    for h in range(HALVES):
        sig_recv[h, pl.ds(p, 1)] = sig_send[h, pl.ds(p, 1)]

    pl.semaphore_wait(barrier, n - 1 + nd - 1)

    def to_peers(src_of, dst, sem):
        def send(i, carry):
            peer = lax.rem(p + i, n)
            pltpu.make_async_remote_copy(
                src_ref=src_of(peer),
                dst_ref=dst.at[p],
                send_sem=send_sems.at[sem],
                recv_sem=recv_sems.at[sem],
                device_id=(peer, d),
                device_id_type=MESH,
            ).start()
            return carry

        lax.fori_loop(1, n, send, 0)

    to_peers(lambda peer: tab_send, tab_recv, 0)
    for h in range(HALVES):
        to_peers(lambda peer, h=h: sig_send.at[h, peer], sig_recv.at[h], 1 + h)

    def await_bytes(ref, sem):
        pltpu.make_async_copy(ref, ref, sem).wait()

    eye = (iota((rows, rows), 0) == iota((rows, rows), 1)).astype(F32).astype(BF16)
    back[...] = dot_nt(eye, pattern[...]).astype(BF16)
    locals_[9].wait()
    unit = iota((8, width), 0)
    mine = (iota((8, width), 1) == unit // KH * (n * KH) + KH * p + lax.rem(unit, KH)) & (
        unit < HALVES * KH
    )
    tap_rows = dot_nt(mine.astype(F32).astype(BF16), filt[...])
    lag = iota((steps, steps), 1) - iota((steps, steps), 0)
    causal = (lag >= 0) & (lag < taps)
    for k in range(HALVES * KH):
        for c in range(TYPES):
            first = c * taps
            base = first // steps * steps
            line = jnp.broadcast_to(tap_rows[k : k + 1, base : base + steps], (steps, steps))
            turned = pltpu.roll(line, (steps - (first - base)) % steps, 1, stride=1, stride_axis=0)
            toep[k, c * steps : (c + 1) * steps, :] = jnp.where(causal, turned, 0.0).astype(BF16)

    await_bytes(tab_recv.at[pl.ds(0, n - 1)], recv_sems.at[0])
    tables = tab_recv[...].astype(F32)
    kind = tables[:, 2, :]
    high = jnp.where(kind >= 2.0, 1.0, 0.0)
    index_b[...] = jnp.where(tables[:, 3, :] > 0.0, high * groups + tables[:, 1, :], -1.0)
    index_s[...] = (kind - 2.0 * high) * groups + tables[:, 0, :]
    wide = iota((2 * groups, slots), 0).astype(F32)

    def count_readers(step, total):
        hot_b, hot_s = [], []
        for j in range(READER_CHUNK):
            r = step * READER_CHUNK + j
            hot_b.append(jnp.where(wide == index_b[pl.ds(r, 1), :], 1.0, 0.0).astype(BF16))
            hot_s.append(jnp.where(wide == index_s[pl.ds(r, 1), :], 1.0, 0.0).astype(BF16))
        return total + dot_nt(jnp.concatenate(hot_b, axis=1), jnp.concatenate(hot_s, axis=1))

    count = lax.fori_loop(
        0, n // READER_CHUNK, count_readers, jnp.zeros((2 * groups, 2 * groups), F32)
    )
    hundreds = jnp.floor(count * (1.0 / 256.0))
    units = count - 256.0 * hundreds
    parts = []
    for c in range(TYPES):
        r0, c0 = c // 2 * groups, c % 2 * groups
        parts.append(
            jnp.concatenate(
                [
                    units[r0 : r0 + groups, c0 : c0 + groups],
                    hundreds[r0 : r0 + groups, c0 : c0 + groups],
                ],
                axis=1,
            )
        )
    counts = jnp.concatenate(parts, axis=0).astype(BF16)

    for h in range(HALVES):
        await_bytes(sig_recv.at[h, pl.ds(0, n - 1)], recv_sems.at[1 + h])
        rows_f[...] = sig_recv[h].astype(F32)
        by_k = []
        for k in range(KH):
            by_k.append(
                jnp.concatenate([rows_f[:, GROUPS_OWN * k + g, :] for g in range(GROUPS_OWN)], axis=0)
            )
        signal = jnp.concatenate(by_k, axis=1)
        signal = jnp.concatenate([signal, 256.0 * signal], axis=0).astype(BF16)
        summed = dot(counts, signal)
        for k in range(KH):
            part = summed[:, k * steps : (k + 1) * steps]
            part = jnp.concatenate([part[c * groups : (c + 1) * groups] for c in range(TYPES)], axis=1)
            upper = part.astype(BF16)
            lower = (part - upper.astype(F32)).astype(BF16)
            both = dot(jnp.concatenate([upper, lower], axis=0), toep[KH * h + k])
            arriving = both[:groups] + both[groups:]
            for g in range(GROUPS_OWN):
                rows_f[:, GROUPS_OWN * k + g, :] = arriving[g * n : (g + 1) * n]
        in_send[h] = rows_f[...].astype(BF16)
        in_recv[h, pl.ds(p, 1)] = in_send[h, pl.ds(p, 1)]
        to_peers(lambda peer, h=h: in_send.at[h, peer], in_recv.at[h], 3 + h)

    total = jnp.zeros((rows, steps), F32)
    for h in range(HALVES):
        await_bytes(in_recv.at[h, pl.ds(0, n - 1)], recv_sems.at[3 + h])
        incoming = in_recv[h].astype(F32).reshape(n * ROWS, steps).astype(BF16)
        total = total + dot(back[:, h * n * ROWS : (h + 1) * n * ROWS], incoming)
    term_send[...] = total.astype(BF16)
    for i in range(1, nd):
        pltpu.make_async_remote_copy(
            src_ref=term_send,
            dst_ref=term_recv.at[d],
            send_sem=send_sems.at[5],
            recv_sem=recv_sems.at[5],
            device_id=(p, lax.rem(d + i, nd)),
            device_id_type=MESH,
        ).start()
    term_recv[pl.ds(d, 1)] = term_send[...][None]
    await_bytes(tab_recv.at[pl.ds(0, n - 1)], send_sems.at[0])
    for h in range(HALVES):
        await_bytes(sig_send.at[h, pl.ds(0, n - 1)], send_sems.at[1 + h])
        await_bytes(in_send.at[h, pl.ds(0, n - 1)], send_sems.at[3 + h])
    await_bytes(term_recv.at[pl.ds(0, nd - 1)], recv_sems.at[5])
    field = term_recv[0].astype(F32)
    for i in range(1, nd):
        field = field + term_recv[i].astype(F32)
    out[...] = field.astype(BF16)
    await_bytes(term_recv.at[pl.ds(0, nd - 1)], send_sems.at[5])


def local(
    currents,
    basis_group,
    projection,
    filters,
    pair_src,
    pair_dst,
    pair_type,
    live_count,
    send_group,
    recv_group,
):
    n = lax.axis_size("grp")
    nd = lax.axis_size("dir")
    rows, steps = currents.shape
    width = projection.shape[1]
    taps = filters.shape[1]
    slots = pair_src.shape[0]
    groups = GROUPS_OWN * n
    any_space = pl.BlockSpec(memory_space=pltpu.HBM)
    return pl.pallas_call(
        functools.partial(kernel, n, nd, taps),
        out_shape=pltpu.VMEM((rows, steps), BF16),
        in_specs=[any_space] * 10,
        out_specs=pl.BlockSpec(memory_space=pltpu.VMEM),
        scratch_shapes=[
            pltpu.VMEM((rows, steps), BF16),
            pltpu.VMEM((1, rows), jnp.int32),
            pltpu.VMEM((rows, width), BF16),
            pltpu.VMEM((TYPES * taps, width), BF16),
            pltpu.VMEM((1, slots), jnp.int32),
            pltpu.VMEM((1, slots), jnp.int32),
            pltpu.VMEM((1, slots), jnp.int32),
            pltpu.VMEM((1, 1), jnp.int32),
            pltpu.VMEM((n, n), jnp.int32),
            pltpu.VMEM((n, n), jnp.int32),
            pltpu.SemaphoreType.DMA((10,)),
            pltpu.VMEM((NTAB, slots), BF16),
            pltpu.VMEM((n, NTAB, slots), BF16),
            pltpu.VMEM((HALVES, n, ROWS, steps), BF16),
            pltpu.VMEM((HALVES, n, ROWS, steps), BF16),
            pltpu.VMEM((HALVES, n, ROWS, steps), BF16),
            pltpu.VMEM((HALVES, n, ROWS, steps), BF16),
            pltpu.VMEM((rows, steps), BF16),
            pltpu.VMEM((nd, rows, steps), BF16),
            pltpu.SemaphoreType.DMA((6,)),
            pltpu.SemaphoreType.DMA((6,)),
            pltpu.VMEM((GROUPS_OWN * width, rows), BF16),
            pltpu.VMEM((rows, GROUPS_OWN * width), BF16),
            pltpu.VMEM((HALVES * KH, TYPES * steps, steps), BF16),
            pltpu.VMEM((n, slots), F32),
            pltpu.VMEM((n, slots), F32),
            pltpu.VMEM((n, ROWS, steps), F32),
        ],
        compiler_params=pltpu.CompilerParams(
            collective_id=0, has_side_effects=True, vmem_limit_bytes=63 * 1024 * 1024
        ),
        name="far_field",
    )(
        currents,
        basis_group.reshape(1, rows),
        projection,
        filters.reshape(TYPES * taps, width),
        pair_src.reshape(1, slots),
        pair_dst.reshape(1, slots),
        pair_type.reshape(1, slots),
        live_count.reshape(1, 1),
        send_group,
        recv_group,
    )


def solution(mesh):
    return jax.shard_map(
        local,
        mesh=mesh,
        in_specs=(
            P("grp", None),
            P("grp"),
            P("grp", "dir"),
            P(None, None, "dir"),
            P("grp"),
            P("grp"),
            P("grp"),
            P("grp"),
            P(),
            P(),
        ),
        out_specs=P("grp", None),
        check_vma=False,
    )
```

```python
import functools

import jax
import jax.numpy as jnp
from jax import lax
from jax.experimental import pallas as pl
from jax.experimental.pallas import tpu as pltpu
from jax.sharding import PartitionSpec as P

MESH = pl.DeviceIdType.MESH
F32 = jnp.float32
BF16 = jnp.bfloat16
TYPES = 4
GROUPS_OWN = 2
HALVES = 2
KH = 2
ROWS = GROUPS_OWN * KH
NTAB = 4
BLOCK = 16


def dot_nt(a, b):
    return lax.dot_general(a, b, (((1,), (1,)), ((), ())), preferred_element_type=F32)


def dot(a, b):
    return jnp.dot(a, b, preferred_element_type=F32)


def iota(shape, axis):
    return lax.broadcasted_iota(jnp.int32, shape, axis)


def kernel(
    n,
    nd,
    taps,
    cur_h,
    bg_h,
    proj_h,
    filt_h,
    src_h,
    dst_h,
    typ_h,
    live_h,
    sg_h,
    rg_h,
    out,
    cur,
    bg,
    proj,
    filt,
    src,
    dst,
    typ,
    live,
    sg,
    rg,
    local_sems,
    tab_send,
    tab_recv,
    sig_send,
    sig_recv,
    in_send,
    in_recv,
    term_send,
    term_recv,
    send_sems,
    recv_sems,
    table_sems,
    pattern,
    back,
    toep,
    rows_f,
):
    p = lax.axis_index("grp")
    d = lax.axis_index("dir")
    rows, steps = cur.shape
    slots = src.shape[1]
    groups = GROUPS_OWN * n

    block = min(BLOCK, n)
    half = block // 2
    lane = p & (block - 1)
    late = jnp.where(lane < half, 0, 1)
    ys = n // block
    z = lane >> 1
    across = [
        (((p // block + r // 2) & (ys - 1)) * block) | ((lane & 1) ^ (r & 1)) for r in range(2 * ys)
    ]

    def each_peer(act):
        def step(u, carry):
            away = half // 2 + jnp.where((u & 1) == 1, (u + 1) >> 1, half - (u >> 1))
            place = ((z + away) & (half - 1)) << 1
            for base in across:
                act(base | place)
            return carry

        lax.fori_loop(0, half - 1, step, 0)
        for base in across[1:]:
            act(base | (z << 1))

    barrier = pltpu.get_barrier_semaphore()
    each_peer(lambda peer: pl.semaphore_signal(barrier, 1, device_id=(peer, d), device_id_type=MESH))
    for i in range(1, nd):
        pl.semaphore_signal(barrier, 1, device_id=(p, lax.rem(d + i, nd)), device_id_type=MESH)

    locals_ = []
    for i, (a, b) in enumerate(
        [
            (src_h, src),
            (dst_h, dst),
            (typ_h, typ),
            (live_h, live),
            (sg_h, sg),
            (rg_h, rg),
            (proj_h, proj),
            (cur_h, cur),
            (bg_h, bg),
            (filt_h, filt),
        ]
    ):
        copy = pltpu.make_async_copy(a, b, local_sems.at[i])
        copy.start()
        locals_.append(copy)

    for copy in locals_[:6]:
        copy.wait()
    owners = iota((n, slots), 0)
    here = iota((n, n), 1) == p
    send_col = jnp.sum(jnp.where(here, sg[...].astype(F32), 0.0), axis=1, keepdims=True)
    recv_col = jnp.sum(jnp.where(here, rg[...].astype(F32), 0.0), axis=1, keepdims=True)
    send_of = jnp.sum(jnp.where(owners == src[...], send_col, 0.0), axis=0, keepdims=True)
    recv_of = jnp.sum(jnp.where(owners == dst[...], recv_col, 0.0), axis=0, keepdims=True)
    source = send_of * n + src[...].astype(F32)
    target = recv_of * n + dst[...].astype(F32)
    is_live = jnp.where(iota((1, slots), 1) < live[...], 1.0, 0.0)
    row = iota((NTAB, slots), 0)
    table = jnp.where(
        row == 0,
        source,
        jnp.where(row == 1, target, jnp.where(row == 2, typ[...].astype(F32), is_live)),
    )
    tab_send[...] = table.astype(BF16)
    tab_recv[pl.ds(p, 1)] = table.astype(BF16)[None]

    for copy in locals_[6:9]:
        copy.wait()
    width = proj.shape[1]
    pick = (iota((GROUPS_OWN * width, width), 0) // GROUPS_OWN == iota((GROUPS_OWN * width, width), 1))
    spread = dot_nt(pick.astype(F32).astype(BF16), proj[...])
    owned = lax.rem(iota((GROUPS_OWN * width, rows), 0), GROUPS_OWN) == bg[...]
    pattern[...] = jnp.where(owned, spread, 0.0).astype(BF16)
    signature = dot(pattern[...], cur[...])
    sig_send[...] = signature.reshape(HALVES, n, ROWS, steps).astype(BF16)
    for h in range(HALVES):
        sig_recv[h, pl.ds(p, 1)] = sig_send[h, pl.ds(p, 1)]

    pl.semaphore_wait(barrier, n - 1 + nd - 1)

    def to_peers(src_of, dst, sem, recv_sem):
        def send(peer):
            pltpu.make_async_remote_copy(
                src_ref=src_of(peer),
                dst_ref=dst.at[p],
                send_sem=send_sems.at[sem],
                recv_sem=recv_sem,
                device_id=(peer, d),
                device_id_type=MESH,
            ).start()

        each_peer(send)

    to_peers(lambda peer: tab_send, tab_recv, 0, table_sems.at[late])
    for h in range(HALVES):
        to_peers(lambda peer, h=h: sig_send.at[h, peer], sig_recv.at[h], 1 + h, recv_sems.at[1 + h])

    def await_bytes(ref, sem):
        pltpu.make_async_copy(ref, ref, sem).wait()

    eye = (iota((rows, rows), 0) == iota((rows, rows), 1)).astype(F32).astype(BF16)
    back[...] = dot_nt(eye, pattern[...]).astype(BF16)
    locals_[9].wait()
    unit = iota((8, width), 0)
    mine = (iota((8, width), 1) == unit // KH * (n * KH) + KH * p + lax.rem(unit, KH)) & (
        unit < HALVES * KH
    )
    tap_rows = dot_nt(mine.astype(F32).astype(BF16), filt[...])
    lag = iota((steps, steps), 1) - iota((steps, steps), 0)
    causal = (lag >= 0) & (lag < taps)
    for k in range(HALVES * KH):
        for c in range(TYPES):
            first = c * taps
            base = first // steps * steps
            line = jnp.broadcast_to(tap_rows[k : k + 1, base : base + steps], (steps, steps))
            turned = pltpu.roll(line, (steps - (first - base)) % steps, 1, stride=1, stride_axis=0)
            toep[k, c * steps : (c + 1) * steps, :] = jnp.where(causal, turned, 0.0).astype(BF16)

    wide = iota((2 * groups, slots), 0).astype(F32).astype(BF16)
    one, none = jnp.ones((), BF16), jnp.zeros((), BF16)

    def hot(index):
        spread = jnp.broadcast_to(index, (2 * groups, slots)).astype(BF16)
        return jnp.where(wide == spread, one, none)

    count = jnp.zeros((2 * groups, 2 * groups), F32)
    for part in (1, 0):

        @pl.when(late == part)
        def _():
            await_bytes(tab_recv.at[pl.ds(0, n // 2 - 1)], table_sems.at[part])

        @pl.when(late != part)
        def _():
            await_bytes(tab_recv.at[pl.ds(0, n // 2)], table_sems.at[part])

        def count_block(y, total):
            readers = pl.ds(y * block + half * part, half)
            tables = tab_recv[readers].astype(F32)
            kind = tables[:, 2, :]
            high = jnp.where(kind >= 2.0, 1.0, 0.0)
            index_b = jnp.where(tables[:, 3, :] > 0.0, high * groups + tables[:, 1, :], -1.0)
            index_s = (kind - 2.0 * high) * groups + tables[:, 0, :]
            hot_b = [hot(index_b[j : j + 1]) for j in range(half)]
            hot_s = [hot(index_s[j : j + 1]) for j in range(half)]
            return total + dot_nt(jnp.concatenate(hot_b, axis=1), jnp.concatenate(hot_s, axis=1))

        count = lax.fori_loop(0, n // block, count_block, count)
    hundreds = jnp.floor(count * (1.0 / 256.0))
    units = count - 256.0 * hundreds
    parts = []
    for c in range(TYPES):
        r0, c0 = c // 2 * groups, c % 2 * groups
        parts.append(
            jnp.concatenate(
                [
                    units[r0 : r0 + groups, c0 : c0 + groups],
                    hundreds[r0 : r0 + groups, c0 : c0 + groups],
                ],
                axis=1,
            )
        )
    counts = jnp.concatenate(parts, axis=0).astype(BF16)

    for h in range(HALVES):
        await_bytes(sig_recv.at[h, pl.ds(0, n - 1)], recv_sems.at[1 + h])
        rows_f[...] = sig_recv[h].astype(F32)
        by_k = []
        for k in range(KH):
            by_k.append(
                jnp.concatenate([rows_f[:, GROUPS_OWN * k + g, :] for g in range(GROUPS_OWN)], axis=0)
            )
        signal = jnp.concatenate(by_k, axis=1)
        signal = jnp.concatenate([signal, 256.0 * signal], axis=0).astype(BF16)
        summed = dot(counts, signal)
        for k in range(KH):
            part = summed[:, k * steps : (k + 1) * steps]
            part = jnp.concatenate([part[c * groups : (c + 1) * groups] for c in range(TYPES)], axis=1)
            upper = part.astype(BF16)
            lower = (part - upper.astype(F32)).astype(BF16)
            both = dot(jnp.concatenate([upper, lower], axis=0), toep[KH * h + k])
            arriving = both[:groups] + both[groups:]
            for g in range(GROUPS_OWN):
                rows_f[:, GROUPS_OWN * k + g, :] = arriving[g * n : (g + 1) * n]
        in_send[h] = rows_f[...].astype(BF16)
        in_recv[h, pl.ds(p, 1)] = in_send[h, pl.ds(p, 1)]
        to_peers(lambda peer, h=h: in_send.at[h, peer], in_recv.at[h], 3 + h, recv_sems.at[3 + h])

    incoming = []
    for h in range(HALVES):
        await_bytes(in_recv.at[h, pl.ds(0, n - 1)], recv_sems.at[3 + h])
        incoming.append(in_recv[h].astype(F32).reshape(n * ROWS, steps).astype(BF16))
    incoming = jnp.concatenate(incoming, axis=0)
    part = rows // 2
    for b in range(2):
        term_send[b] = dot(back[b * part : (b + 1) * part], incoming).astype(BF16)
        for i in (2, 1, 3) if nd == 4 else range(1, nd):
            pltpu.make_async_remote_copy(
                src_ref=term_send.at[b],
                dst_ref=term_recv.at[b, d],
                send_sem=send_sems.at[5 + b],
                recv_sem=recv_sems.at[5 + b],
                device_id=(p, lax.rem(d + i, nd)),
                device_id_type=MESH,
            ).start()
        term_recv[b, pl.ds(d, 1)] = term_send[b][None]
    await_bytes(tab_recv.at[pl.ds(0, n - 1)], send_sems.at[0])
    for h in range(HALVES):
        await_bytes(sig_send.at[h, pl.ds(0, n - 1)], send_sems.at[1 + h])
        await_bytes(in_send.at[h, pl.ds(0, n - 1)], send_sems.at[3 + h])
    for b in range(2):
        await_bytes(term_recv.at[b, pl.ds(0, nd - 1)], recv_sems.at[5 + b])
        field = term_recv[b, 0].astype(F32)
        for i in range(1, nd):
            field = field + term_recv[b, i].astype(F32)
        out[b * part : (b + 1) * part, :] = field.astype(BF16)
        await_bytes(term_recv.at[b, pl.ds(0, nd - 1)], send_sems.at[5 + b])


def local(
    currents,
    basis_group,
    projection,
    filters,
    pair_src,
    pair_dst,
    pair_type,
    live_count,
    send_group,
    recv_group,
):
    n = lax.axis_size("grp")
    nd = lax.axis_size("dir")
    rows, steps = currents.shape
    width = projection.shape[1]
    taps = filters.shape[1]
    slots = pair_src.shape[0]
    groups = GROUPS_OWN * n
    any_space = pl.BlockSpec(memory_space=pltpu.HBM)
    return pl.pallas_call(
        functools.partial(kernel, n, nd, taps),
        out_shape=pltpu.VMEM((rows, steps), BF16),
        in_specs=[any_space] * 10,
        out_specs=pl.BlockSpec(memory_space=pltpu.VMEM),
        scratch_shapes=[
            pltpu.VMEM((rows, steps), BF16),
            pltpu.VMEM((1, rows), jnp.int32),
            pltpu.VMEM((rows, width), BF16),
            pltpu.VMEM((TYPES * taps, width), BF16),
            pltpu.VMEM((1, slots), jnp.int32),
            pltpu.VMEM((1, slots), jnp.int32),
            pltpu.VMEM((1, slots), jnp.int32),
            pltpu.VMEM((1, 1), jnp.int32),
            pltpu.VMEM((n, n), jnp.int32),
            pltpu.VMEM((n, n), jnp.int32),
            pltpu.SemaphoreType.DMA((10,)),
            pltpu.VMEM((NTAB, slots), BF16),
            pltpu.VMEM((n, NTAB, slots), BF16),
            pltpu.VMEM((HALVES, n, ROWS, steps), BF16),
            pltpu.VMEM((HALVES, n, ROWS, steps), BF16),
            pltpu.VMEM((HALVES, n, ROWS, steps), BF16),
            pltpu.VMEM((HALVES, n, ROWS, steps), BF16),
            pltpu.VMEM((2, rows // 2, steps), BF16),
            pltpu.VMEM((2, nd, rows // 2, steps), BF16),
            pltpu.SemaphoreType.DMA((7,)),
            pltpu.SemaphoreType.DMA((7,)),
            pltpu.SemaphoreType.DMA((2,)),
            pltpu.VMEM((GROUPS_OWN * width, rows), BF16),
            pltpu.VMEM((rows, GROUPS_OWN * width), BF16),
            pltpu.VMEM((HALVES * KH, TYPES * steps, steps), BF16),
            pltpu.VMEM((n, ROWS, steps), F32),
        ],
        compiler_params=pltpu.CompilerParams(
            collective_id=0, has_side_effects=True, vmem_limit_bytes=63 * 1024 * 1024
        ),
        name="far_field",
    )(
        currents,
        basis_group.reshape(1, rows),
        projection,
        filters.reshape(TYPES * taps, width),
        pair_src.reshape(1, slots),
        pair_dst.reshape(1, slots),
        pair_type.reshape(1, slots),
        live_count.reshape(1, 1),
        send_group,
        recv_group,
    )


def solution(mesh):
    return jax.shard_map(
        local,
        mesh=mesh,
        in_specs=(
            P("grp", None),
            P("grp"),
            P("grp", "dir"),
            P(None, None, "dir"),
            P("grp"),
            P("grp"),
            P("grp"),
            P("grp"),
            P(),
            P(),
        ),
        out_specs=P("grp", None),
        check_vma=False,
    )
```

```python
import functools

import jax
import jax.numpy as jnp
from jax import lax
from jax.experimental import pallas as pl
from jax.experimental.pallas import tpu as pltpu
from jax.sharding import PartitionSpec as P

MESH = pl.DeviceIdType.MESH
F32 = jnp.float32
BF16 = jnp.bfloat16
TYPES = 4
GROUPS_OWN = 2
HALVES = 2
KH = 2
ROWS = GROUPS_OWN * KH
NTAB = 4
BLOCK = 16


def dot_nt(a, b):
    return lax.dot_general(a, b, (((1,), (1,)), ((), ())), preferred_element_type=F32)


def dot(a, b):
    return jnp.dot(a, b, preferred_element_type=F32)


def iota(shape, axis):
    return lax.broadcasted_iota(jnp.int32, shape, axis)


def kernel(
    n,
    nd,
    taps,
    cur_h,
    bg_h,
    proj_h,
    filt_h,
    src_h,
    dst_h,
    typ_h,
    live_h,
    sg_h,
    rg_h,
    out,
    cur,
    bg,
    proj,
    filt,
    src,
    dst,
    typ,
    live,
    sg,
    rg,
    local_sems,
    tab_send,
    tab_recv,
    sig_send,
    sig_recv,
    in_send,
    in_recv,
    term_send,
    term_recv,
    send_sems,
    recv_sems,
    table_sems,
    pattern,
    back,
    toep,
    rows_f,
):
    p = lax.axis_index("grp")
    d = lax.axis_index("dir")
    rows, steps = cur.shape
    slots = src.shape[1]
    groups = GROUPS_OWN * n

    block = min(BLOCK, n)
    half = block // 2
    lane = p & (block - 1)
    late = jnp.where(lane < half, 0, 1)
    ys = n // block
    z = lane >> 1
    across = [
        (((p // block + r // 2) & (ys - 1)) * block) | ((lane & 1) ^ (r & 1)) for r in range(2 * ys)
    ]

    def each_peer(act):
        zs = [((z + i) & (half - 1)) << 1 for i in range(half)]
        offs = [(a, r) for a in range(half) for r in range(2 * ys)][1:]
        zd = lambda a: min(a, half - a)
        yd = lambda r: min(r // 2, ys - r // 2)
        offs.sort(key=lambda t: -(zd(t[0]) + yd(t[1])))
        for a, r in offs:
            act(across[r] | zs[a])

    barrier = pltpu.get_barrier_semaphore()
    each_peer(lambda peer: pl.semaphore_signal(barrier, 1, device_id=(peer, d), device_id_type=MESH))
    for i in range(1, nd):
        pl.semaphore_signal(barrier, 1, device_id=(p, lax.rem(d + i, nd)), device_id_type=MESH)

    locals_ = []
    for i, (a, b) in enumerate(
        [
            (src_h, src),
            (dst_h, dst),
            (typ_h, typ),
            (live_h, live),
            (sg_h, sg),
            (rg_h, rg),
            (proj_h, proj),
            (cur_h, cur),
            (bg_h, bg),
            (filt_h, filt),
        ]
    ):
        copy = pltpu.make_async_copy(a, b, local_sems.at[i])
        copy.start()
        locals_.append(copy)

    for copy in locals_[:6]:
        copy.wait()
    owners = iota((n, slots), 0)
    here = iota((n, n), 1) == p
    send_col = jnp.sum(jnp.where(here, sg[...].astype(F32), 0.0), axis=1, keepdims=True)
    recv_col = jnp.sum(jnp.where(here, rg[...].astype(F32), 0.0), axis=1, keepdims=True)
    send_of = jnp.sum(jnp.where(owners == src[...], send_col, 0.0), axis=0, keepdims=True)
    recv_of = jnp.sum(jnp.where(owners == dst[...], recv_col, 0.0), axis=0, keepdims=True)
    source = send_of * n + src[...].astype(F32)
    target = recv_of * n + dst[...].astype(F32)
    is_live = jnp.where(iota((1, slots), 1) < live[...], 1.0, 0.0)
    row = iota((NTAB, slots), 0)
    table = jnp.where(
        row == 0,
        source,
        jnp.where(row == 1, target, jnp.where(row == 2, typ[...].astype(F32), is_live)),
    )
    tab_send[...] = table.astype(BF16)
    tab_recv[pl.ds(p, 1)] = table.astype(BF16)[None]

    for copy in locals_[6:9]:
        copy.wait()
    width = proj.shape[1]
    pick = (iota((GROUPS_OWN * width, width), 0) // GROUPS_OWN == iota((GROUPS_OWN * width, width), 1))
    spread = dot_nt(pick.astype(F32).astype(BF16), proj[...])
    owned = lax.rem(iota((GROUPS_OWN * width, rows), 0), GROUPS_OWN) == bg[...]
    pattern[...] = jnp.where(owned, spread, 0.0).astype(BF16)
    signature = dot(pattern[...], cur[...])
    split = steps // 2
    low, high = signature[: n * ROWS], signature[n * ROWS :]
    for h in range(HALVES):
        span = slice(h * split, (h + 1) * split)
        packed = jnp.concatenate([low[:, span], high[:, span]], axis=1)
        sig_send[h] = packed.reshape(n, ROWS, steps).astype(BF16)
        sig_recv[h, pl.ds(p, 1)] = sig_send[h, pl.ds(p, 1)]

    pl.semaphore_wait(barrier, n - 1 + nd - 1)

    def to_peers(src_of, dst, sem, recv_sem):
        def send(peer):
            pltpu.make_async_remote_copy(
                src_ref=src_of(peer),
                dst_ref=dst.at[p],
                send_sem=send_sems.at[sem],
                recv_sem=recv_sem,
                device_id=(peer, d),
                device_id_type=MESH,
            ).start()

        each_peer(send)

    to_peers(lambda peer: tab_send, tab_recv, 0, table_sems.at[late])
    for h in range(HALVES):
        to_peers(lambda peer, h=h: sig_send.at[h, peer], sig_recv.at[h], 1 + h, recv_sems.at[1 + h])

    def await_bytes(ref, sem):
        pltpu.make_async_copy(ref, ref, sem).wait()

    eye = (iota((rows, rows), 0) == iota((rows, rows), 1)).astype(F32).astype(BF16)
    back[...] = dot_nt(eye, pattern[...]).astype(BF16)
    locals_[9].wait()
    unit = iota((8, width), 0)
    mine = (iota((8, width), 1) == unit // KH * (n * KH) + KH * p + lax.rem(unit, KH)) & (
        unit < HALVES * KH
    )
    tap_rows = dot_nt(mine.astype(F32).astype(BF16), filt[...])
    lag = iota((split, steps), 1) - iota((split, steps), 0)
    causal = (lag >= 0) & (lag < taps)
    left = iota((split, steps), 1) < split
    for unit in range(HALVES * KH):
        side, k = unit // KH, unit % KH
        for c in range(TYPES):
            first = c * taps
            base = first // steps * steps
            line = jnp.broadcast_to(tap_rows[unit : unit + 1, base : base + steps], (split, steps))
            turned = pltpu.roll(line, (steps - (first - base)) % steps, 1, stride=1, stride_axis=0)
            wide = jnp.where(causal, turned, 0.0)
            crossed = pltpu.roll(wide, split, 1)
            here = left if side == 0 else jnp.logical_not(left)
            same, next_half = (wide, crossed) if side == 0 else (crossed, wide)
            at = pl.ds(c * steps + side * split, split)
            toep[k, at, :] = jnp.where(here, same, 0.0).astype(BF16)
            toep[KH + k, at, :] = jnp.where(here, next_half, 0.0).astype(BF16)

    wide = iota((2 * groups, slots), 0).astype(F32).astype(BF16)
    one, none = jnp.ones((), BF16), jnp.zeros((), BF16)

    def hot(index):
        spread = jnp.broadcast_to(index, (2 * groups, slots)).astype(BF16)
        return jnp.where(wide == spread, one, none)

    count = jnp.zeros((2 * groups, 2 * groups), F32)
    for part in (1, 0):

        @pl.when(late == part)
        def _():
            await_bytes(tab_recv.at[pl.ds(0, n // 2 - 1)], table_sems.at[part])

        @pl.when(late != part)
        def _():
            await_bytes(tab_recv.at[pl.ds(0, n // 2)], table_sems.at[part])

        def count_block(y, total):
            readers = pl.ds(y * block + half * part, half)
            tables = tab_recv[readers].astype(F32)
            kind = tables[:, 2, :]
            high = jnp.where(kind >= 2.0, 1.0, 0.0)
            index_b = jnp.where(tables[:, 3, :] > 0.0, high * groups + tables[:, 1, :], -1.0)
            index_s = (kind - 2.0 * high) * groups + tables[:, 0, :]
            hot_b = [hot(index_b[j : j + 1]) for j in range(half)]
            hot_s = [hot(index_s[j : j + 1]) for j in range(half)]
            return total + dot_nt(jnp.concatenate(hot_b, axis=1), jnp.concatenate(hot_s, axis=1))

        count = lax.fori_loop(0, n // block, count_block, count)
    hundreds = jnp.floor(count * (1.0 / 256.0))
    units = count - 256.0 * hundreds
    parts = []
    for c in range(TYPES):
        r0, c0 = c // 2 * groups, c % 2 * groups
        parts.append(
            jnp.concatenate(
                [
                    units[r0 : r0 + groups, c0 : c0 + groups],
                    hundreds[r0 : r0 + groups, c0 : c0 + groups],
                ],
                axis=1,
            )
        )
    counts = jnp.concatenate(parts, axis=0).astype(BF16)

    earlier = []
    for h in range(HALVES):
        await_bytes(sig_recv.at[h, pl.ds(0, n - 1)], recv_sems.at[1 + h])
        rows_f[...] = sig_recv[h].astype(F32)
        by_k = []
        for k in range(KH):
            by_k.append(
                jnp.concatenate([rows_f[:, GROUPS_OWN * k + g, :] for g in range(GROUPS_OWN)], axis=0)
            )
        signal = jnp.concatenate(by_k, axis=1)
        signal = jnp.concatenate([signal, 256.0 * signal], axis=0).astype(BF16)
        summed = dot(counts, signal)
        for k in range(KH):
            part = summed[:, k * steps : (k + 1) * steps]
            part = jnp.concatenate([part[c * groups : (c + 1) * groups] for c in range(TYPES)], axis=1)
            upper = part.astype(BF16)
            lower = (part - upper.astype(F32)).astype(BF16)
            parts = jnp.concatenate([upper, lower], axis=0)
            both = dot(parts, toep[k])
            if h == 0:
                earlier.append(parts)
            else:
                both = both + dot(earlier[k], toep[KH + k])
            arriving = both[:groups] + both[groups:]
            for g in range(GROUPS_OWN):
                rows_f[:, GROUPS_OWN * k + g, :] = arriving[g * n : (g + 1) * n]
        in_send[h] = rows_f[...].astype(BF16)
        in_recv[h, pl.ds(p, 1)] = in_send[h, pl.ds(p, 1)]
        to_peers(lambda peer, h=h: in_send.at[h, peer], in_recv.at[h], 3 + h, recv_sems.at[3 + h])

    part = rows // 2
    on_left = iota((part, steps), 1) < split
    for h in range(HALVES):
        await_bytes(in_recv.at[h, pl.ds(0, n - 1)], recv_sems.at[3 + h])
        incoming = in_recv[h].astype(F32).reshape(n * ROWS, steps).astype(BF16)
        of_low = dot(back[:, : n * ROWS], incoming)
        of_high = dot(back[:, n * ROWS :], incoming)
        upper = of_low[:part] + pltpu.roll(of_high[:part], split, 1)
        lower = pltpu.roll(of_low[part:], split, 1) + of_high[part:]
        term_send[h] = jnp.where(on_left, upper, lower).astype(BF16)
        for i in (2, 1, 3) if nd == 4 else range(1, nd):
            pltpu.make_async_remote_copy(
                src_ref=term_send.at[h],
                dst_ref=term_recv.at[h, d],
                send_sem=send_sems.at[5 + h],
                recv_sem=recv_sems.at[5 + h],
                device_id=(p, lax.rem(d + i, nd)),
                device_id_type=MESH,
            ).start()
        term_recv[h, pl.ds(d, 1)] = term_send[h][None]
    await_bytes(tab_recv.at[pl.ds(0, n - 1)], send_sems.at[0])
    for h in range(HALVES):
        await_bytes(sig_send.at[h, pl.ds(0, n - 1)], send_sems.at[1 + h])
        await_bytes(in_send.at[h, pl.ds(0, n - 1)], send_sems.at[3 + h])
    fields = []
    for h in range(HALVES):
        await_bytes(term_recv.at[h, pl.ds(0, nd - 1)], recv_sems.at[5 + h])
        field = term_recv[h, 0].astype(F32)
        for i in range(1, nd):
            field = field + term_recv[h, i].astype(F32)
        fields.append(field)
        await_bytes(term_recv.at[h, pl.ds(0, nd - 1)], send_sems.at[5 + h])
    out[:part, :] = jnp.where(on_left, fields[0], pltpu.roll(fields[1], split, 1)).astype(BF16)
    out[part:, :] = jnp.where(on_left, pltpu.roll(fields[0], split, 1), fields[1]).astype(BF16)


def local(
    currents,
    basis_group,
    projection,
    filters,
    pair_src,
    pair_dst,
    pair_type,
    live_count,
    send_group,
    recv_group,
):
    n = lax.axis_size("grp")
    nd = lax.axis_size("dir")
    rows, steps = currents.shape
    width = projection.shape[1]
    taps = filters.shape[1]
    slots = pair_src.shape[0]
    groups = GROUPS_OWN * n
    any_space = pl.BlockSpec(memory_space=pltpu.HBM)
    return pl.pallas_call(
        functools.partial(kernel, n, nd, taps),
        out_shape=pltpu.VMEM((rows, steps), BF16),
        in_specs=[any_space] * 10,
        out_specs=pl.BlockSpec(memory_space=pltpu.VMEM),
        scratch_shapes=[
            pltpu.VMEM((rows, steps), BF16),
            pltpu.VMEM((1, rows), jnp.int32),
            pltpu.VMEM((rows, width), BF16),
            pltpu.VMEM((TYPES * taps, width), BF16),
            pltpu.VMEM((1, slots), jnp.int32),
            pltpu.VMEM((1, slots), jnp.int32),
            pltpu.VMEM((1, slots), jnp.int32),
            pltpu.VMEM((1, 1), jnp.int32),
            pltpu.VMEM((n, n), jnp.int32),
            pltpu.VMEM((n, n), jnp.int32),
            pltpu.SemaphoreType.DMA((10,)),
            pltpu.VMEM((NTAB, slots), BF16),
            pltpu.VMEM((n, NTAB, slots), BF16),
            pltpu.VMEM((HALVES, n, ROWS, steps), BF16),
            pltpu.VMEM((HALVES, n, ROWS, steps), BF16),
            pltpu.VMEM((HALVES, n, ROWS, steps), BF16),
            pltpu.VMEM((HALVES, n, ROWS, steps), BF16),
            pltpu.VMEM((2, rows // 2, steps), BF16),
            pltpu.VMEM((2, nd, rows // 2, steps), BF16),
            pltpu.SemaphoreType.DMA((7,)),
            pltpu.SemaphoreType.DMA((7,)),
            pltpu.SemaphoreType.DMA((2,)),
            pltpu.VMEM((GROUPS_OWN * width, rows), BF16),
            pltpu.VMEM((rows, GROUPS_OWN * width), BF16),
            pltpu.VMEM((HALVES * KH, TYPES * steps, steps), BF16),
            pltpu.VMEM((n, ROWS, steps), F32),
        ],
        compiler_params=pltpu.CompilerParams(
            collective_id=0, has_side_effects=True, vmem_limit_bytes=63 * 1024 * 1024
        ),
        name="far_field",
    )(
        currents,
        basis_group.reshape(1, rows),
        projection,
        filters.reshape(TYPES * taps, width),
        pair_src.reshape(1, slots),
        pair_dst.reshape(1, slots),
        pair_type.reshape(1, slots),
        live_count.reshape(1, 1),
        send_group,
        recv_group,
    )


def solution(mesh):
    return jax.shard_map(
        local,
        mesh=mesh,
        in_specs=(
            P("grp", None),
            P("grp"),
            P("grp", "dir"),
            P(None, None, "dir"),
            P("grp"),
            P("grp"),
            P("grp"),
            P("grp"),
            P(),
            P(),
        ),
        out_specs=P("grp", None),
        check_vma=False,
    )
```

```python
import functools

import jax
import jax.numpy as jnp
from jax import lax
from jax.experimental import pallas as pl
from jax.experimental.pallas import tpu as pltpu
from jax.sharding import PartitionSpec as P

MESH = pl.DeviceIdType.MESH
F32 = jnp.float32
BF16 = jnp.bfloat16
TYPES = 4
GROUPS_OWN = 2
HALVES = 2
KH = 2
ROWS = GROUPS_OWN * KH
NTAB = 4
BLOCK = 16


def dot_nt(a, b):
    return lax.dot_general(a, b, (((1,), (1,)), ((), ())), preferred_element_type=F32)


def dot(a, b):
    return jnp.dot(a, b, preferred_element_type=F32)


def iota(shape, axis):
    return lax.broadcasted_iota(jnp.int32, shape, axis)


def kernel(
    n,
    nd,
    taps,
    cur_h,
    bg_h,
    proj_h,
    filt_h,
    src_h,
    dst_h,
    typ_h,
    live_h,
    sg_h,
    rg_h,
    out,
    cur,
    bg,
    proj,
    filt,
    src,
    dst,
    typ,
    live,
    sg,
    rg,
    local_sems,
    tab_send,
    tab_recv,
    sig_send,
    sig_recv,
    in_send,
    in_recv,
    term_send,
    term_recv,
    send_sems,
    recv_sems,
    table_sems,
    pattern,
    back,
    toep,
    rows_f,
):
    p = lax.axis_index("grp")
    d = lax.axis_index("dir")
    rows, steps = cur.shape
    slots = src.shape[1]
    groups = GROUPS_OWN * n

    block = min(BLOCK, n)
    half = block // 2
    lane = p & (block - 1)
    late = jnp.where(lane < half, 0, 1)
    ys = n // block
    z = lane >> 1
    across = [
        (((p // block + r // 2) & (ys - 1)) * block) | ((lane & 1) ^ (r & 1)) for r in range(2 * ys)
    ]

    def each_peer(act):
        zs = [((z + i) & (half - 1)) << 1 for i in range(half)]
        offs = [(a, r) for a in range(half) for r in range(2 * ys)][1:]
        zd = lambda a: min(a, half - a)
        yd = lambda r: min(r // 2, ys - r // 2)
        offs.sort(key=lambda t: -(2 * zd(t[0]) + yd(t[1])))
        for a, r in offs:
            act(across[r] | zs[a])

    locals_ = []
    for i, (a, b) in enumerate(
        [
            (src_h, src),
            (dst_h, dst),
            (typ_h, typ),
            (live_h, live),
            (sg_h, sg),
            (rg_h, rg),
            (proj_h, proj),
            (cur_h, cur),
            (bg_h, bg),
            (filt_h, filt),
        ]
    ):
        copy = pltpu.make_async_copy(a, b, local_sems.at[i])
        copy.start()
        locals_.append(copy)

    barrier = pltpu.get_barrier_semaphore()
    each_peer(lambda peer: pl.semaphore_signal(barrier, 1, device_id=(peer, d), device_id_type=MESH))
    for i in range(1, nd):
        pl.semaphore_signal(barrier, 1, device_id=(p, lax.rem(d + i, nd)), device_id_type=MESH)

    for copy in locals_[:6]:
        copy.wait()
    owners = iota((n, slots), 0)
    here = iota((n, n), 1) == p
    send_col = jnp.sum(jnp.where(here, sg[...].astype(F32), 0.0), axis=1, keepdims=True)
    recv_col = jnp.sum(jnp.where(here, rg[...].astype(F32), 0.0), axis=1, keepdims=True)
    send_of = jnp.sum(jnp.where(owners == src[...], send_col, 0.0), axis=0, keepdims=True)
    recv_of = jnp.sum(jnp.where(owners == dst[...], recv_col, 0.0), axis=0, keepdims=True)
    source = send_of * n + src[...].astype(F32)
    target = recv_of * n + dst[...].astype(F32)
    is_live = jnp.where(iota((1, slots), 1) < live[...], 1.0, 0.0)
    row = iota((NTAB, slots), 0)
    table = jnp.where(
        row == 0,
        source,
        jnp.where(row == 1, target, jnp.where(row == 2, typ[...].astype(F32), is_live)),
    )
    tab_send[...] = table.astype(BF16)
    tab_recv[pl.ds(p, 1)] = table.astype(BF16)[None]

    for copy in locals_[6:9]:
        copy.wait()
    width = proj.shape[1]
    pick = (iota((GROUPS_OWN * width, width), 0) // GROUPS_OWN == iota((GROUPS_OWN * width, width), 1))
    spread = dot_nt(pick.astype(F32).astype(BF16), proj[...])
    owned = lax.rem(iota((GROUPS_OWN * width, rows), 0), GROUPS_OWN) == bg[...]
    pattern[...] = jnp.where(owned, spread, 0.0).astype(BF16)
    signature = dot(pattern[...], cur[...])
    split = steps // 2
    low, high = signature[: n * ROWS], signature[n * ROWS :]
    for h in range(HALVES):
        span = slice(h * split, (h + 1) * split)
        packed = jnp.concatenate([low[:, span], high[:, span]], axis=1)
        sig_send[h] = packed.reshape(n, ROWS, steps).astype(BF16)
        sig_recv[h, pl.ds(p, 1)] = sig_send[h, pl.ds(p, 1)]

    pl.semaphore_wait(barrier, n - 1 + nd - 1)

    def to_peers(src_of, dst, sem, recv_sem):
        def send(peer):
            pltpu.make_async_remote_copy(
                src_ref=src_of(peer),
                dst_ref=dst.at[p],
                send_sem=send_sems.at[sem],
                recv_sem=recv_sem,
                device_id=(peer, d),
                device_id_type=MESH,
            ).start()

        each_peer(send)

    to_peers(lambda peer: tab_send, tab_recv, 0, table_sems.at[late])
    for h in range(HALVES):
        to_peers(lambda peer, h=h: sig_send.at[h, peer], sig_recv.at[h], 1 + h, recv_sems.at[1 + h])

    def await_bytes(ref, sem):
        pltpu.make_async_copy(ref, ref, sem).wait()

    eye = (iota((rows, rows), 0) == iota((rows, rows), 1)).astype(F32).astype(BF16)
    back[...] = dot_nt(eye, pattern[...]).astype(BF16)
    locals_[9].wait()
    unit = iota((8, width), 0)
    mine = (iota((8, width), 1) == unit // KH * (n * KH) + KH * p + lax.rem(unit, KH)) & (
        unit < HALVES * KH
    )
    tap_rows = dot_nt(mine.astype(F32).astype(BF16), filt[...])
    lag = iota((split, steps), 1) - iota((split, steps), 0)
    causal = (lag >= 0) & (lag < taps)
    left = iota((split, steps), 1) < split
    for unit in range(HALVES * KH):
        side, k = unit // KH, unit % KH
        for c in range(TYPES):
            first = c * taps
            base = first // steps * steps
            line = jnp.broadcast_to(tap_rows[unit : unit + 1, base : base + steps], (split, steps))
            turned = pltpu.roll(line, (steps - (first - base)) % steps, 1, stride=1, stride_axis=0)
            wide = jnp.where(causal, turned, 0.0)
            crossed = pltpu.roll(wide, split, 1)
            here = left if side == 0 else jnp.logical_not(left)
            same, next_half = (wide, crossed) if side == 0 else (crossed, wide)
            at = pl.ds(c * steps + side * split, split)
            toep[k, at, :] = jnp.where(here, same, 0.0).astype(BF16)
            toep[KH + k, at, :] = jnp.where(here, next_half, 0.0).astype(BF16)

    wide = iota((2 * groups, slots), 0).astype(F32).astype(BF16)
    one, none = jnp.ones((), BF16), jnp.zeros((), BF16)

    def hot(index):
        spread = jnp.broadcast_to(index, (2 * groups, slots)).astype(BF16)
        return jnp.where(wide == spread, one, none)

    count = jnp.zeros((2 * groups, 2 * groups), F32)
    for part in (1, 0):

        @pl.when(late == part)
        def _():
            await_bytes(tab_recv.at[pl.ds(0, n // 2 - 1)], table_sems.at[part])

        @pl.when(late != part)
        def _():
            await_bytes(tab_recv.at[pl.ds(0, n // 2)], table_sems.at[part])

        def count_block(y, total):
            readers = pl.ds(y * block + half * part, half)
            tables = tab_recv[readers].astype(F32)
            kind = tables[:, 2, :]
            high = jnp.where(kind >= 2.0, 1.0, 0.0)
            index_b = jnp.where(tables[:, 3, :] > 0.0, high * groups + tables[:, 1, :], -1.0)
            index_s = (kind - 2.0 * high) * groups + tables[:, 0, :]
            hot_b = [hot(index_b[j : j + 1]) for j in range(half)]
            hot_s = [hot(index_s[j : j + 1]) for j in range(half)]
            return total + dot_nt(jnp.concatenate(hot_b, axis=1), jnp.concatenate(hot_s, axis=1))

        count = lax.fori_loop(0, n // block, count_block, count)
    hundreds = jnp.floor(count * (1.0 / 256.0))
    units = count - 256.0 * hundreds
    parts = []
    for c in range(TYPES):
        r0, c0 = c // 2 * groups, c % 2 * groups
        parts.append(
            jnp.concatenate(
                [
                    units[r0 : r0 + groups, c0 : c0 + groups],
                    hundreds[r0 : r0 + groups, c0 : c0 + groups],
                ],
                axis=1,
            )
        )
    counts = jnp.concatenate(parts, axis=0).astype(BF16)

    earlier = []
    for h in range(HALVES):
        await_bytes(sig_recv.at[h, pl.ds(0, n - 1)], recv_sems.at[1 + h])
        rows_f[...] = sig_recv[h].astype(F32)
        by_k = []
        for k in range(KH):
            by_k.append(
                jnp.concatenate([rows_f[:, GROUPS_OWN * k + g, :] for g in range(GROUPS_OWN)], axis=0)
            )
        signal = jnp.concatenate(by_k, axis=1)
        signal = jnp.concatenate([signal, 256.0 * signal], axis=0).astype(BF16)
        summed = dot(counts, signal)
        for k in range(KH):
            part = summed[:, k * steps : (k + 1) * steps]
            part = jnp.concatenate([part[c * groups : (c + 1) * groups] for c in range(TYPES)], axis=1)
            upper = part.astype(BF16)
            lower = (part - upper.astype(F32)).astype(BF16)
            parts = jnp.concatenate([upper, lower], axis=0)
            both = dot(parts, toep[k])
            if h == 0:
                earlier.append(parts)
            else:
                both = both + dot(earlier[k], toep[KH + k])
            arriving = both[:groups] + both[groups:]
            for g in range(GROUPS_OWN):
                rows_f[:, GROUPS_OWN * k + g, :] = arriving[g * n : (g + 1) * n]
        in_send[h] = rows_f[...].astype(BF16)
        in_recv[h, pl.ds(p, 1)] = in_send[h, pl.ds(p, 1)]
        to_peers(lambda peer, h=h: in_send.at[h, peer], in_recv.at[h], 3 + h, recv_sems.at[3 + h])

    part = rows // 2
    on_left = iota((part, steps), 1) < split
    for h in range(HALVES):
        await_bytes(in_recv.at[h, pl.ds(0, n - 1)], recv_sems.at[3 + h])
        incoming = in_recv[h].astype(F32).reshape(n * ROWS, steps).astype(BF16)
        of_low = dot(back[:, : n * ROWS], incoming)
        of_high = dot(back[:, n * ROWS :], incoming)
        upper = of_low[:part] + pltpu.roll(of_high[:part], split, 1)
        lower = pltpu.roll(of_low[part:], split, 1) + of_high[part:]
        term_send[h] = jnp.where(on_left, upper, lower).astype(BF16)
        for i in (2, 1, 3) if nd == 4 else range(1, nd):
            pltpu.make_async_remote_copy(
                src_ref=term_send.at[h],
                dst_ref=term_recv.at[h, d],
                send_sem=send_sems.at[5 + h],
                recv_sem=recv_sems.at[5 + h],
                device_id=(p, lax.rem(d + i, nd)),
                device_id_type=MESH,
            ).start()
        term_recv[h, pl.ds(d, 1)] = term_send[h][None]
    fields = []
    for h in range(HALVES):
        await_bytes(term_recv.at[h, pl.ds(0, nd - 1)], recv_sems.at[5 + h])
        field = term_recv[h, 0].astype(F32)
        for i in range(1, nd):
            field = field + term_recv[h, i].astype(F32)
        fields.append(field)
    out[:part, :] = jnp.where(on_left, fields[0], pltpu.roll(fields[1], split, 1)).astype(BF16)
    out[part:, :] = jnp.where(on_left, pltpu.roll(fields[0], split, 1), fields[1]).astype(BF16)
    await_bytes(tab_recv.at[pl.ds(0, n - 1)], send_sems.at[0])
    for h in range(HALVES):
        await_bytes(sig_send.at[h, pl.ds(0, n - 1)], send_sems.at[1 + h])
        await_bytes(in_send.at[h, pl.ds(0, n - 1)], send_sems.at[3 + h])
        await_bytes(term_recv.at[h, pl.ds(0, nd - 1)], send_sems.at[5 + h])


def local(
    currents,
    basis_group,
    projection,
    filters,
    pair_src,
    pair_dst,
    pair_type,
    live_count,
    send_group,
    recv_group,
):
    n = lax.axis_size("grp")
    nd = lax.axis_size("dir")
    rows, steps = currents.shape
    width = projection.shape[1]
    taps = filters.shape[1]
    slots = pair_src.shape[0]
    groups = GROUPS_OWN * n
    any_space = pl.BlockSpec(memory_space=pltpu.HBM)
    return pl.pallas_call(
        functools.partial(kernel, n, nd, taps),
        out_shape=pltpu.VMEM((rows, steps), BF16),
        in_specs=[any_space] * 10,
        out_specs=pl.BlockSpec(memory_space=pltpu.VMEM),
        scratch_shapes=[
            pltpu.VMEM((rows, steps), BF16),
            pltpu.VMEM((1, rows), jnp.int32),
            pltpu.VMEM((rows, width), BF16),
            pltpu.VMEM((TYPES * taps, width), BF16),
            pltpu.VMEM((1, slots), jnp.int32),
            pltpu.VMEM((1, slots), jnp.int32),
            pltpu.VMEM((1, slots), jnp.int32),
            pltpu.VMEM((1, 1), jnp.int32),
            pltpu.VMEM((n, n), jnp.int32),
            pltpu.VMEM((n, n), jnp.int32),
            pltpu.SemaphoreType.DMA((10,)),
            pltpu.VMEM((NTAB, slots), BF16),
            pltpu.VMEM((n, NTAB, slots), BF16),
            pltpu.VMEM((HALVES, n, ROWS, steps), BF16),
            pltpu.VMEM((HALVES, n, ROWS, steps), BF16),
            pltpu.VMEM((HALVES, n, ROWS, steps), BF16),
            pltpu.VMEM((HALVES, n, ROWS, steps), BF16),
            pltpu.VMEM((2, rows // 2, steps), BF16),
            pltpu.VMEM((2, nd, rows // 2, steps), BF16),
            pltpu.SemaphoreType.DMA((7,)),
            pltpu.SemaphoreType.DMA((7,)),
            pltpu.SemaphoreType.DMA((2,)),
            pltpu.VMEM((GROUPS_OWN * width, rows), BF16),
            pltpu.VMEM((rows, GROUPS_OWN * width), BF16),
            pltpu.VMEM((HALVES * KH, TYPES * steps, steps), BF16),
            pltpu.VMEM((n, ROWS, steps), F32),
        ],
        compiler_params=pltpu.CompilerParams(
            collective_id=0, has_side_effects=True, vmem_limit_bytes=63 * 1024 * 1024
        ),
        name="far_field",
    )(
        currents,
        basis_group.reshape(1, rows),
        projection,
        filters.reshape(TYPES * taps, width),
        pair_src.reshape(1, slots),
        pair_dst.reshape(1, slots),
        pair_type.reshape(1, slots),
        live_count.reshape(1, 1),
        send_group,
        recv_group,
    )


def solution(mesh):
    return jax.shard_map(
        local,
        mesh=mesh,
        in_specs=(
            P("grp", None),
            P("grp"),
            P("grp", "dir"),
            P(None, None, "dir"),
            P("grp"),
            P("grp"),
            P("grp"),
            P("grp"),
            P(),
            P(),
        ),
        out_specs=P("grp", None),
        check_vma=False,
    )
```
